768 devices in a mesh: pair: 48 (over z, x_hi, core), blk: 8 (over y), rep: 2 (over x_lo).
Axes of the slice: x: 4 (x_hi: 2, x_lo: 2; x = x_hi * 2 + x_lo), y: 8, z: 12, core: 2. Of those that a mesh axis runs over, the one named last changes fastest.
Arguments:
- amplitudes: bfloat16 [6144, 6144], P('pair'), may hold values from -6 to 6
- tile_map: int32 [48, 48], replicated, may hold values 0 or 1
- ladder_ints: bfloat16 [6144, 48, 128], P('rep', None, 'blk'), may hold values from -0.078125 to 0.078125
- hole_ints: bfloat16 [48, 128, 6144], P(None, ('blk', 'rep')), may hold values from -0.078125 to 0.078125
Outputs:
- residual: bfloat16 [48, 48, 128, 128], P('pair', None, ('blk', 'rep'))
The draws below stay inside these ranges and needn't reach their ends.
Inputs may be any that keep to these rules, and one draw needn't show every extreme that they name: tile_map holds only 0 and 1.
All inputs are finite; a program needn't handle non-finite values.
Results may differ from the reference program's by a relative error of at most 0.001.
Values may be sent and summed in bfloat16 or wider, within the bound.
A program may use at most 32 MiB of HBM per device.

```python
import jax
import jax.numpy as jnp

TS = 128
OPD = 128
NTILES = 48
NOP = 6144
NVP = 6144
N_PAIR = 48


def place_ends(values, key, least, high):
    spot = [jax.random.randint(jax.random.fold_in(key, axis), (), 0, length) for axis, length in enumerate(values.shape)]
    longest = values.shape.index(max(values.shape))
    neighbour = spot[:longest] + [(spot[longest] + 1) % values.shape[longest]] + spot[longest + 1:]
    return values.at[tuple(spot)].set(least).at[tuple(neighbour)].set(high)


def shard_levels(stream_key, extent, shards, least, largest):
    gain = 1.0
    for axis_at, blocks in shards:
        draws = jax.random.uniform(jax.random.fold_in(jax.random.fold_in(stream_key, 6), axis_at), (blocks,), jnp.float32, least / len(shards), largest / len(shards))
        gain = gain * jnp.repeat(jnp.exp(draws), extent[axis_at] // blocks).reshape((-1,) + (1,) * (len(extent) - 1 - axis_at))
    return gain


def normal_values(own_key, extent, deviation, reach, pieces=(), held_as=jnp.bfloat16):
    level = shard_levels(own_key, extent, pieces, -0.22, 0.18) if pieces else 1.0
    result = jax.random.normal(own_key, extent, jnp.float32) * deviation * level
    return jnp.minimum(jnp.maximum(result, -reach), reach).astype(held_as)


def setup_inputs(seed: int = 0) -> dict:
    key_of = jax.random.split(jax.random.key(seed), 5)
    amplitudes = normal_values(key_of[0], (NOP, NVP), 1.0, 6.0, ((0, 48),))
    tile_map = place_ends((jax.random.randint(key_of[1], (NTILES, NTILES), 0, 4) < 3).astype(jnp.int32), jax.random.fold_in(key_of[1], 1), 0, 1)
    ladder_ints = normal_values(key_of[2], (NVP, NTILES, TS), NVP ** -0.5, 0.078125, ((0, 2), (2, 8)))
    hole_ints = normal_values(key_of[3], (N_PAIR, OPD, NOP), NOP ** -0.5, 0.078125, ((1, 16),))
    return dict(amplitudes=amplitudes, tile_map=tile_map, ladder_ints=ladder_ints, hole_ints=hole_ints)


def tile_order(tile_map):
    counts = jnp.sum(tile_map, axis=0).astype(jnp.int32)
    tile_ids = jnp.arange(tile_map.shape[1], dtype=jnp.int32)
    scores = counts * tile_map.shape[1] + tile_ids
    return jnp.argsort(-scores, stable=True).astype(jnp.int32)


def reference(amplitudes, tile_map, ladder_ints, hole_ints):
    blocks = amplitudes.reshape(N_PAIR, OPD, NTILES, TS)
    kept_tiles = tile_map.astype(amplitudes.dtype)[:, None, :, None]
    masked = (blocks * kept_tiles).reshape(NOP, NVP)
    widened = masked.astype(jnp.float32)
    particle = jnp.dot(widened, ladder_ints.reshape(NVP, NVP).astype(jnp.float32), preferred_element_type=jnp.float32)
    holes = jnp.dot(hole_ints.reshape(NOP, NOP).astype(jnp.float32), widened, preferred_element_type=jnp.float32)
    combined = (particle + holes).astype(jnp.bfloat16).reshape(N_PAIR, OPD, NTILES, TS)
    chosen_blocks = tile_order(tile_map)
    taken = jnp.take(combined, chosen_blocks, axis=2)
    return jnp.transpose(taken, (2, 0, 1, 3))
```

```python
import functools

import jax
import jax.numpy as jnp
from jax import lax
from jax.experimental import pallas as pl
from jax.experimental.pallas import tpu as pltpu
from jax.sharding import PartitionSpec as P

MESH = pl.DeviceIdType.MESH
F32 = jnp.float32
BF16 = jnp.bfloat16


def tile_order_and_mask(tm_ref, pair_index, tiles):
    tm = tm_ref[...]
    lane = lax.broadcasted_iota(jnp.int32, (tiles, tiles), 1)
    sub = lax.broadcasted_iota(jnp.int32, (tiles, tiles), 0)
    score_row = jnp.sum(tm, axis=0, keepdims=True) * tiles + lane[:1]
    spread = jnp.broadcast_to(score_row, (tiles, tiles))
    score_col = jnp.sum(jnp.where(lane == sub, spread, 0), axis=1, keepdims=True)
    rank_col = jnp.sum((spread > score_col).astype(jnp.int32), axis=1, keepdims=True)
    order_row = jnp.sum(jnp.where(rank_col == lane, sub, 0), axis=0, keepdims=True)
    mask_row = tm_ref[pl.ds(pair_index, 1), :]
    mask_col = jnp.sum(
        jnp.where(lane == sub, jnp.broadcast_to(mask_row, (tiles, tiles)), 0), axis=1, keepdims=True)
    kept_row = jnp.sum(jnp.where(rank_col == lane, mask_col, 0), axis=0, keepdims=True)
    return order_row, mask_row, kept_row


def swap_lane_blocks(rows, block):
    n = len(rows)
    width = n * block
    lane = lax.broadcasted_iota(jnp.int32, rows[0].shape, 1) // block
    d = n // 2
    while d:
        keep = (lane & d) == 0
        out = list(rows)
        for a in range(n):
            if a & d:
                continue
            b = a + d
            out[a] = jnp.where(keep, rows[a], pltpu.roll(rows[b], d * block, 1))
            out[b] = jnp.where(keep, pltpu.roll(rows[a], width - d * block, 1), rows[b])
        rows = out
        d //= 2
    return rows


def kernel(dims, a_hbm, tm_hbm, l_hbm, h_hbm, out_ref,
           a_ref, tm_ref, l_ref, h_ref, am_ref, meta_ref, meta_smem,
           hsend, panel, psend, prep, ysend, yrecv, vt, qsend, pfin,
           load_sem, meta_sem, h1_send, h1_recv, x_send, x_recv, ring_send, ring_recv,
           p2_send, p2_recv, p3_send, p3_recv, p4_send, p4_recv):
    tiles, n_blk, share, width = dims
    half_tiles = tiles // 2
    p = lax.axis_index("pair")
    y = lax.axis_index("blk")
    x = lax.axis_index("rep")
    core = lax.rem(p, 2)
    zz = p // 2
    other_x = 1 - x
    up = lax.rem(y + 1, n_blk)
    down = lax.rem(y + n_blk - 1, n_blk)

    loads = [
        pltpu.make_async_copy(tm_hbm, tm_ref, load_sem.at[0]),
        pltpu.make_async_copy(l_hbm, l_ref, load_sem.at[1]),
        pltpu.make_async_copy(h_hbm, h_ref, load_sem.at[2]),
    ]
    loads[0].start()

    @pl.loop(0, tiles)
    def _(v):
        start = pl.multiple_of(v * width, width)
        pltpu.make_async_copy(a_hbm.at[:, pl.ds(start, width)], a_ref.at[v], load_sem.at[3]).start()

    loads[1].start()
    loads[2].start()

    barrier = pltpu.get_barrier_semaphore()

    @pl.loop(1, tiles)
    def _(j):
        q = lax.rem(p + j, tiles)
        pl.semaphore_signal(barrier, inc=1, device_id=(q, y, x), device_id_type=MESH)

    @pl.loop(1, n_blk)
    def _(j):
        pl.semaphore_signal(barrier, inc=1, device_id=(p, lax.rem(y + j, n_blk), x), device_id_type=MESH)

    pl.semaphore_signal(barrier, inc=1, device_id=(p, y, other_x), device_id_type=MESH)

    loads[0].wait()
    order_row, mask_row, kept_row = tile_order_and_mask(tm_ref, p, tiles)
    meta_ref[0:1, 0:tiles] = order_row
    meta_ref[1:2, 0:tiles] = mask_row
    meta_ref[2:3, 0:tiles] = kept_row
    to_smem = pltpu.make_async_copy(meta_ref, meta_smem, meta_sem)
    to_smem.start()
    to_smem.wait()
    pltpu.make_async_copy(a_ref, a_ref, load_sem.at[3]).wait()

    parity = lax.rem(core + x, 2)
    rows16 = pl.ds(pl.multiple_of(y * 16, 16), 16)
    for j in range(half_tiles):
        piece = a_ref[meta_smem[0, 2 * j + parity], rows16, :]
        kept = meta_smem[2, 2 * j + parity].astype(F32)
        hsend[j] = (piece.astype(F32) * kept).astype(BF16)

    pl.semaphore_wait(barrier, tiles - 1 + n_blk - 1 + 1)

    @pl.when(x == 0)
    def _():
        pltpu.make_async_copy(hsend.at[zz], panel.at[x, y, zz], h1_recv).start()

    @pl.when(x != 0)
    def _():
        pltpu.make_async_remote_copy(
            hsend.at[zz], panel.at[x, y, zz], h1_send, h1_recv,
            device_id=(2 * zz + parity, y, x), device_id_type=MESH).start()

    @pl.loop(1, half_tiles)
    def _(j):
        dest = lax.rem(zz + j, half_tiles)
        pltpu.make_async_remote_copy(
            hsend.at[dest], panel.at[x, y, zz], h1_send, h1_recv,
            device_id=(2 * dest + parity, y, x), device_id_type=MESH).start()

    for j in range(half_tiles):
        kept = meta_smem[1, x * half_tiles + j].astype(F32)
        am_ref[:, j * width:(j + 1) * width] = (
            a_ref[x * half_tiles + j].astype(F32) * kept).astype(BF16)
    loads[1].wait()
    cols = tiles * share
    step_cols = 256
    for n in range(cols // step_cols):
        part = lax.dot_general(
            am_ref[...], l_ref[n * step_cols:(n + 1) * step_cols, :],
            (((1,), (1,)), ((), ())), preferred_element_type=F32)
        part = part.reshape(n_blk, 2, 8, step_cols)
        for s in range(2):
            psend[s, :, :, n * step_cols:(n + 1) * step_cols] = part[:, s]
    p2 = pltpu.make_async_remote_copy(
        psend.at[other_x], prep, p2_send, p2_recv,
        device_id=(p, y, other_x), device_id_type=MESH)
    p2.start()

    def slot(origin_x, origin_y):
        return panel.at[origin_x, lax.rem(origin_y + 2 * n_blk, n_blk)]

    def ring(step, part, direction):
        origin = x if part == 0 else other_x
        at = y - (step - 1) if direction == 0 else y + (step - 1)
        which = ((step - 1) * 2 + part) * 2 + direction
        return pltpu.make_async_remote_copy(
            slot(origin, at), slot(origin, at), ring_send.at[which], ring_recv.at[which],
            device_id=(p, up if direction == 0 else down, x), device_id_type=MESH)

    copies = {}

    def go(step, part, direction):
        if step > 1:
            copies[(step - 1, part, direction)].wait_recv()
        copies[(step, part, direction)] = ring(step, part, direction)
        copies[(step, part, direction)].start()

    mine = panel.at[x, y]
    pltpu.make_async_copy(mine, mine, h1_recv).wait()
    swap = pltpu.make_async_remote_copy(
        mine, mine, x_send, x_recv, device_id=(p, y, other_x), device_id_type=MESH)
    swap.start()
    go(1, 0, 0)
    go(1, 0, 1)
    swap.wait_recv()
    go(1, 1, 0)
    go(1, 1, 1)

    p2.wait_recv()
    ysend[...] = psend[x] + prep[...]

    @pl.loop(1, n_blk)
    def _(j):
        dest = lax.rem(y + j, n_blk)
        pltpu.make_async_remote_copy(
            ysend.at[dest], yrecv.at[y], p3_send, p3_recv,
            device_id=(p, dest, x), device_id_type=MESH).start()

    pltpu.make_async_copy(ysend.at[y], yrecv.at[y], p3_recv).start()

    for part in range(2):
        for direction in range(2):
            go(2, part, direction)

    pltpu.make_async_copy(yrecv, yrecv, p3_recv).wait()
    per = width // share
    for g in range(cols // width):
        rows = [yrecv[b, :, g * width:(g + 1) * width] for b in range(n_blk)]
        for k, row in enumerate(swap_lane_blocks(rows, share)):
            vt[g * per + k] = row
    for q in range(tiles):
        qsend[q] = vt[meta_smem[0, q]]

    @pl.loop(1, tiles)
    def _(j):
        q = lax.rem(p + j, tiles)
        pltpu.make_async_remote_copy(
            qsend.at[q], pfin.at[p], p4_send, p4_recv,
            device_id=(q, y, x), device_id_type=MESH).start()

    pltpu.make_async_copy(qsend.at[p], pfin.at[p], p4_recv).start()

    for part in range(2):
        for direction in range(2):
            go(3, part, direction)
    go(4, 0, 0)
    go(4, 1, 1)
    copies[(3, 0, 1)].wait_recv()
    copies[(3, 1, 0)].wait_recv()
    copies[(4, 0, 0)].wait_recv()
    copies[(4, 1, 1)].wait_recv()
    loads[2].wait()
    rows_out = out_ref.shape[0]
    acc = jnp.zeros((rows_out, width), F32)
    for j in range(half_tiles):
        even = panel[core, :, j].reshape(width, width)
        odd = panel[1 - core, :, j].reshape(width, width)
        acc += jnp.dot(
            h_ref[:, 2 * j * width:2 * (j + 1) * width],
            jnp.concatenate([even, odd], axis=0), preferred_element_type=F32)

    pltpu.make_async_copy(pfin, pfin, p4_recv).wait()
    out_ref[...] = (acc + pfin[...].reshape(rows_out, width)).astype(BF16)

    @pl.when(x == 0)
    def _():
        sent = hsend.at[pl.ds(0, half_tiles - 1)]
        pltpu.make_async_copy(sent, sent, h1_send).wait()

    @pl.when(x != 0)
    def _():
        pltpu.make_async_copy(hsend, hsend, h1_send).wait()

    swap.wait_send()
    p2.wait_send()
    for copy in copies.values():
        copy.wait_send()
    sent = ysend.at[pl.ds(0, n_blk - 1)]
    pltpu.make_async_copy(sent, sent, p3_send).wait()
    sent = qsend.at[pl.ds(0, tiles - 1)]
    pltpu.make_async_copy(sent, sent, p4_send).wait()


def per_device(amplitudes, tile_map, ladder_ints, hole_ints):
    rows, total = amplitudes.shape
    tiles = tile_map.shape[0]
    width = total // tiles
    half_rows, _, share = ladder_ints.shape
    n_blk = width // share
    local_rows = hole_ints.shape[1]
    ladder = jnp.transpose(ladder_ints, (1, 2, 0)).reshape(tiles * share, half_rows)
    holes = hole_ints.reshape(tiles * local_rows, hole_ints.shape[2])
    dma = pltpu.SemaphoreType.DMA
    out = pl.pallas_call(
        functools.partial(kernel, (tiles, n_blk, share, width)),
        out_shape=jax.ShapeDtypeStruct((tiles * local_rows, width), BF16),
        in_specs=[pl.BlockSpec(memory_space=pl.ANY)] * 4,
        out_specs=pl.BlockSpec(memory_space=pltpu.VMEM),
        scratch_shapes=[
            pltpu.VMEM((tiles, rows, width), BF16),
            pltpu.VMEM((tiles, tiles), jnp.int32),
            pltpu.VMEM(ladder.shape, BF16),
            pltpu.VMEM(holes.shape, BF16),
            pltpu.VMEM((rows, half_rows), BF16),
            pltpu.VMEM((8, 128), jnp.int32),
            pltpu.SMEM((8, 128), jnp.int32),
            pltpu.VMEM((tiles // 2, 16, width), BF16),
            pltpu.VMEM((2, n_blk, tiles // 2, 16, width), BF16),
            pltpu.VMEM((2, n_blk, 8, tiles * share), F32),
            pltpu.VMEM((n_blk, 8, tiles * share), F32),
            pltpu.VMEM((n_blk, 8, tiles * share), F32),
            pltpu.VMEM((n_blk, 8, tiles * share), F32),
            pltpu.VMEM((tiles, 8, width), F32),
            pltpu.VMEM((tiles, 8, width), F32),
            pltpu.VMEM((tiles, 8, width), F32),
            dma((4,)), dma(()), dma(()), dma(()), dma(()), dma(()), dma((16,)), dma((16,)),
            dma(()), dma(()), dma(()), dma(()), dma(()), dma(()),
        ],
        compiler_params=pltpu.CompilerParams(
            collective_id=0, has_side_effects=True, vmem_limit_bytes=32 * 1024 * 1024),
        cost_estimate=pl.CostEstimate(flops=1_300_000_000, bytes_accessed=12_000_000, transcendentals=0),
    )(amplitudes, tile_map, ladder, holes)
    return out.reshape(1, tiles, local_rows, width)


def solution(mesh):
    placed = (P("pair", None), P(), P("rep", None, "blk"), P(None, ("blk", "rep"), None))
    return jax.shard_map(
        per_device,
        mesh=mesh,
        in_specs=placed,
        out_specs=P("pair", None, ("blk", "rep"), None),
        check_vma=False,
    )
```

```python
import functools

import jax
import jax.numpy as jnp
from jax import lax
from jax.experimental import pallas as pl
from jax.experimental.pallas import tpu as pltpu
from jax.sharding import PartitionSpec as P

MESH = pl.DeviceIdType.MESH
F32 = jnp.float32
BF16 = jnp.bfloat16


def tile_order_and_mask(tm_ref, pair_index, tiles):
    tm = tm_ref[...]
    lane = lax.broadcasted_iota(jnp.int32, (tiles, tiles), 1)
    sub = lax.broadcasted_iota(jnp.int32, (tiles, tiles), 0)
    score_row = jnp.sum(tm, axis=0, keepdims=True) * tiles + lane[:1]
    spread = jnp.broadcast_to(score_row, (tiles, tiles))
    score_col = jnp.sum(jnp.where(lane == sub, spread, 0), axis=1, keepdims=True)
    rank_col = jnp.sum((spread > score_col).astype(jnp.int32), axis=1, keepdims=True)
    order_row = jnp.sum(jnp.where(rank_col == lane, sub, 0), axis=0, keepdims=True)
    mask_row = tm_ref[pl.ds(pair_index, 1), :]
    mask_col = jnp.sum(
        jnp.where(lane == sub, jnp.broadcast_to(mask_row, (tiles, tiles)), 0), axis=1, keepdims=True)
    kept_row = jnp.sum(jnp.where(rank_col == lane, mask_col, 0), axis=0, keepdims=True)
    return order_row, mask_row, kept_row


def swap_lane_blocks(rows, block):
    n = len(rows)
    width = n * block
    lane = lax.broadcasted_iota(jnp.int32, rows[0].shape, 1) // block
    d = n // 2
    while d:
        keep = (lane & d) == 0
        out = list(rows)
        for a in range(n):
            if a & d:
                continue
            b = a + d
            out[a] = jnp.where(keep, rows[a], pltpu.roll(rows[b], d * block, 1))
            out[b] = jnp.where(keep, pltpu.roll(rows[a], width - d * block, 1), rows[b])
        rows = out
        d //= 2
    return rows


def kernel(dims, a_hbm, tm_hbm, l_hbm, h_hbm, out_ref,
           a_ref, tm_ref, l_ref, h_ref, am_ref, lg_ref, meta_ref, meta_smem,
           hsend, panel, psend, prep, ysend, yrecv, qsend, pfin,
           load_sem, meta_sem, h1_send, h1_recv, ring_send, ring_recv,
           p2_send, p2_recv, p3_send, p3_recv, p4_send, p4_recv):
    tiles, n_blk, share, width = dims
    half_tiles = tiles // 2
    p = lax.axis_index("pair")
    y = lax.axis_index("blk")
    x = lax.axis_index("rep")
    core = lax.rem(p, 2)
    zz = p // 2
    other_x = 1 - x
    up = lax.rem(y + 1, n_blk)
    down = lax.rem(y + n_blk - 1, n_blk)

    loads = [
        pltpu.make_async_copy(tm_hbm, tm_ref, load_sem.at[0]),
        pltpu.make_async_copy(l_hbm, l_ref, load_sem.at[1]),
        pltpu.make_async_copy(h_hbm, h_ref, load_sem.at[2]),
    ]
    loads[0].start()

    @pl.loop(0, tiles)
    def _(v):
        start = pl.multiple_of(v * width, width)
        pltpu.make_async_copy(a_hbm.at[:, pl.ds(start, width)], a_ref.at[v], load_sem.at[3]).start()

    loads[1].start()

    barrier = pltpu.get_barrier_semaphore()

    @pl.loop(1, tiles)
    def _(j):
        q = lax.rem(p + j, tiles)
        pl.semaphore_signal(barrier, inc=1, device_id=(q, y, x), device_id_type=MESH)

    @pl.loop(1, n_blk)
    def _(j):
        pl.semaphore_signal(barrier, inc=1, device_id=(p, lax.rem(y + j, n_blk), x), device_id_type=MESH)

    pl.semaphore_signal(barrier, inc=1, device_id=(p, y, other_x), device_id_type=MESH)

    loads[0].wait()
    order_row, mask_row, kept_row = tile_order_and_mask(tm_ref, p, tiles)
    meta_ref[0:1, 0:tiles] = order_row
    meta_ref[1:2, 0:tiles] = mask_row
    meta_ref[2:3, 0:tiles] = kept_row
    to_smem = pltpu.make_async_copy(meta_ref, meta_smem, meta_sem)
    to_smem.start()
    to_smem.wait()
    pltpu.make_async_copy(a_ref, a_ref, load_sem.at[3]).wait()

    parity = lax.rem(core + x, 2)
    rows16 = pl.ds(pl.multiple_of(y * 16, 16), 16)
    for j in range(half_tiles):
        piece = a_ref[meta_smem[0, 2 * j + parity], rows16, :]
        kept = meta_smem[2, 2 * j + parity].astype(F32)
        hsend[j] = (piece.astype(F32) * kept).astype(BF16)

    pl.semaphore_wait(barrier, tiles - 1 + n_blk - 1 + 1)

    chunk = half_tiles // 2

    @pl.when(x == 0)
    def _():
        pltpu.make_async_copy(hsend.at[zz], panel.at[x, y, 0], h1_recv.at[0]).start()

    @pl.when(x != 0)
    def _():
        pltpu.make_async_remote_copy(
            hsend.at[zz], panel.at[x, y, 0], h1_send, h1_recv.at[0],
            device_id=(2 * zz + parity, y, x), device_id_type=MESH).start()

    for c in range(2):
        @pl.loop(max(1, c * chunk), (c + 1) * chunk)
        def _(k):
            dest = lax.rem(zz + jnp.where(lax.rem(k, 2) == 1, (k + 1) // 2, half_tiles - k // 2), half_tiles)
            pltpu.make_async_remote_copy(
                hsend.at[dest], panel.at[x, y, k], h1_send, h1_recv.at[c],
                device_id=(2 * dest + parity, y, x), device_id_type=MESH).start()

    loads[2].start()

    groups = 3
    per_group = tiles // groups
    step_cols = per_group * share

    def entry(n, pos):
        return 4 * groups * (pos // 4) + 4 * n + pos % 4

    for j in range(half_tiles):
        kept = meta_smem[1, x * half_tiles + j].astype(F32)
        am_ref[:, j * width:(j + 1) * width] = (
            a_ref[x * half_tiles + j].astype(F32) * kept).astype(BF16)
    loads[1].wait()
    p2 = []
    for n in range(groups):
        for pos in range(per_group):
            lg_ref[n, pos * share:(pos + 1) * share, :] = l_ref[meta_smem[0, entry(n, pos)]]
        part = lax.dot_general(
            am_ref[...], lg_ref[n], (((1,), (1,)), ((), ())), preferred_element_type=F32)
        part = part.reshape(n_blk, 2, 8, step_cols)
        for s in range(2):
            psend[n, s] = part[:, s]
        p2.append(pltpu.make_async_remote_copy(
            psend.at[n, other_x], prep.at[n], p2_send.at[n], p2_recv.at[n],
            device_id=(p, y, other_x), device_id_type=MESH))
        p2[n].start()

    copies = {}

    def slot(origin_x, origin_y, first, count):
        return panel.at[origin_x, lax.rem(origin_y + 2 * n_blk, n_blk), pl.ds(first, count)]

    def send(key, ref, to_y, to_x):
        which = len(copies)
        copies[key] = pltpu.make_async_remote_copy(
            ref, ref, ring_send.at[which], ring_recv.at[which],
            device_id=(p, to_y, to_x), device_id_type=MESH)
        copies[key].start()

    def spread_chunk0(step):
        for d in range(2):
            if step > 1:
                copies[("near", step - 1, d)].wait_recv()
            origin = y - (step - 1) if d == 0 else y + (step - 1)
            arrived = slot(x, origin, 0, chunk)
            if step < 4:
                send(("near", step, d), arrived, up if d == 0 else down, x)
            elif step == 4:
                send(("near", step, d), slot(x, origin, d * (chunk // 2), chunk // 2), up if d == 0 else down, x)
            else:
                arrived = slot(x, origin, d * (chunk // 2), chunk // 2)
            if step > 1 or d == 0:
                send(("over", step, d), arrived, y, other_x)

    def spread_chunk1(step, part):
        origin_x = x if part == 0 else other_x
        for d in range(2):
            if step > 1:
                copies[("far", step - 1, part, d)].wait_recv()
            if step == 4 and d != part:
                continue
            origin = y - (step - 1) if d == 0 else y + (step - 1)
            send(("far", step, part, d), slot(origin_x, origin, chunk, chunk), up if d == 0 else down, x)

    def particle_rows(n):
        p2[n].wait_recv()
        ysend[n] = psend[n, x] + prep[n]

        @pl.loop(1, n_blk)
        def _(j):
            dest = lax.rem(y + j, n_blk)
            pltpu.make_async_remote_copy(
                ysend.at[n, dest], yrecv.at[n, y], p3_send.at[n], p3_recv.at[n],
                device_id=(p, dest, x), device_id_type=MESH).start()

        pltpu.make_async_copy(ysend.at[n, y], yrecv.at[n, y], p3_recv.at[n]).start()

    def particle_tiles(n):
        pltpu.make_async_copy(yrecv.at[n], yrecv.at[n], p3_recv.at[n]).wait()
        per = width // share
        for g in range(step_cols // width):
            rows = [yrecv[n, b, :, g * width:(g + 1) * width] for b in range(n_blk)]
            for k, row in enumerate(swap_lane_blocks(rows, share)):
                qsend[entry(n, g * per + k)] = row

        @pl.loop(0, per_group)
        def _(j):
            pos = lax.rem(j + p, per_group)
            q = 4 * groups * (pos // 4) + 4 * n + lax.rem(pos, 4)

            @pl.when(q != p)
            def _():
                pltpu.make_async_remote_copy(
                    qsend.at[q], pfin.at[p], p4_send, p4_recv,
                    device_id=(q, y, x), device_id_type=MESH).start()

            @pl.when(q == p)
            def _():
                pltpu.make_async_copy(qsend.at[q], pfin.at[p], p4_recv).start()

    def pieces_in(c):
        mine = panel.at[x, y, pl.ds(c * chunk, chunk)]
        pltpu.make_async_copy(mine, mine, h1_recv.at[c]).wait()

    pieces_in(0)
    spread_chunk0(1)
    particle_rows(0)
    pieces_in(1)
    send(("swap",), slot(x, y, chunk, chunk), y, other_x)
    spread_chunk1(1, 0)
    spread_chunk0(2)
    particle_rows(1)
    copies[("swap",)].wait_recv()
    spread_chunk1(1, 1)
    spread_chunk0(3)
    particle_rows(2)
    particle_tiles(0)
    spread_chunk1(2, 0)
    spread_chunk0(4)
    spread_chunk1(2, 1)
    particle_tiles(1)
    spread_chunk0(5)
    spread_chunk1(3, 0)
    spread_chunk1(3, 1)
    particle_tiles(2)
    spread_chunk1(4, 0)
    spread_chunk1(4, 1)

    rows_out = out_ref.shape[0]

    def product(c, acc):
        for k in range(c * chunk, (c + 1) * chunk):
            offset = (k + 1) // 2 if k % 2 else half_tiles - k // 2
            source = lax.rem(zz + 2 * half_tiles - offset, half_tiles)
            even = panel[core, :, k].reshape(width, width)
            odd = panel[1 - core, :, k].reshape(width, width)
            acc += jnp.dot(
                h_ref[:, pl.ds(pl.multiple_of(source * 2 * width, 2 * width), 2 * width)],
                jnp.concatenate([even, odd], axis=0), preferred_element_type=F32)
        return acc

    loads[2].wait()
    for key, copy in copies.items():
        if key[0] == "over":
            copy.wait_recv()
    acc = product(0, jnp.zeros((rows_out, width), F32))
    copies[("far", 4, 0, 0)].wait_recv()
    copies[("far", 4, 1, 1)].wait_recv()
    acc = product(1, acc)
    pltpu.make_async_copy(pfin, pfin, p4_recv).wait()
    out_ref[...] = (acc + pfin[...].reshape(rows_out, width)).astype(BF16)

    @pl.when(x == 0)
    def _():
        sent = hsend.at[pl.ds(0, half_tiles - 1)]
        pltpu.make_async_copy(sent, sent, h1_send).wait()

    @pl.when(x != 0)
    def _():
        pltpu.make_async_copy(hsend, hsend, h1_send).wait()

    for copy in list(copies.values()) + p2:
        copy.wait_send()
    for n in range(groups):
        sent = ysend.at[n, pl.ds(0, n_blk - 1)]
        pltpu.make_async_copy(sent, sent, p3_send.at[n]).wait()
    sent = qsend.at[pl.ds(0, tiles - 1)]
    pltpu.make_async_copy(sent, sent, p4_send).wait()


def per_device(amplitudes, tile_map, ladder_ints, hole_ints):
    rows, total = amplitudes.shape
    tiles = tile_map.shape[0]
    width = total // tiles
    half_rows, _, share = ladder_ints.shape
    n_blk = width // share
    local_rows = hole_ints.shape[1]
    ladder = jnp.transpose(ladder_ints, (1, 2, 0))
    holes = hole_ints.reshape(tiles * local_rows, hole_ints.shape[2])
    dma = pltpu.SemaphoreType.DMA
    out = pl.pallas_call(
        functools.partial(kernel, (tiles, n_blk, share, width)),
        out_shape=jax.ShapeDtypeStruct((tiles * local_rows, width), BF16),
        in_specs=[pl.BlockSpec(memory_space=pl.ANY)] * 4,
        out_specs=pl.BlockSpec(memory_space=pltpu.VMEM),
        scratch_shapes=[
            pltpu.VMEM((tiles, rows, width), BF16),
            pltpu.VMEM((tiles, tiles), jnp.int32),
            pltpu.VMEM(ladder.shape, BF16),
            pltpu.VMEM(holes.shape, BF16),
            pltpu.VMEM((rows, half_rows), BF16),
            pltpu.VMEM((3, tiles * share // 3, half_rows), BF16),
            pltpu.VMEM((8, 128), jnp.int32),
            pltpu.SMEM((8, 128), jnp.int32),
            pltpu.VMEM((tiles // 2, 16, width), BF16),
            pltpu.VMEM((2, n_blk, tiles // 2, 16, width), BF16),
            pltpu.VMEM((3, 2, n_blk, 8, tiles * share // 3), F32),
            pltpu.VMEM((3, n_blk, 8, tiles * share // 3), F32),
            pltpu.VMEM((3, n_blk, 8, tiles * share // 3), F32),
            pltpu.VMEM((3, n_blk, 8, tiles * share // 3), F32),
            pltpu.VMEM((tiles, 8, width), F32),
            pltpu.VMEM((tiles, 8, width), F32),
            dma((4,)), dma(()), dma(()), dma((2,)), dma((32,)), dma((32,)),
            dma((3,)), dma((3,)), dma((3,)), dma((3,)), dma(()), dma(()),
        ],
        compiler_params=pltpu.CompilerParams(
            collective_id=0, has_side_effects=True, vmem_limit_bytes=60 * 1024 * 1024),
        cost_estimate=pl.CostEstimate(flops=1_300_000_000, bytes_accessed=12_000_000, transcendentals=0),
    )(amplitudes, tile_map, ladder, holes)
    return out.reshape(1, tiles, local_rows, width)


def solution(mesh):
    placed = (P("pair", None), P(), P("rep", None, "blk"), P(None, ("blk", "rep"), None))
    return jax.shard_map(
        per_device,
        mesh=mesh,
        in_specs=placed,
        out_specs=P("pair", None, ("blk", "rep"), None),
        check_vma=False,
    )
```

```python
import functools

import jax
import jax.numpy as jnp
from jax import lax
from jax.experimental import pallas as pl
from jax.experimental.pallas import tpu as pltpu
from jax.sharding import PartitionSpec as P

MESH = pl.DeviceIdType.MESH
F32 = jnp.float32
BF16 = jnp.bfloat16


def tile_order_and_mask(tm_ref, pair_index, tiles):
    tm = tm_ref[...]
    lane = lax.broadcasted_iota(jnp.int32, (tiles, tiles), 1)
    sub = lax.broadcasted_iota(jnp.int32, (tiles, tiles), 0)
    score_row = jnp.sum(tm, axis=0, keepdims=True) * tiles + lane[:1]
    spread = jnp.broadcast_to(score_row, (tiles, tiles))
    score_col = jnp.sum(jnp.where(lane == sub, spread, 0), axis=1, keepdims=True)
    rank_col = jnp.sum((spread > score_col).astype(jnp.int32), axis=1, keepdims=True)
    order_row = jnp.sum(jnp.where(rank_col == lane, sub, 0), axis=0, keepdims=True)
    return order_row, tm_ref[pl.ds(pair_index, 1), :]


def swap_lane_blocks(rows, block):
    n = len(rows)
    width = n * block
    lane = lax.broadcasted_iota(jnp.int32, rows[0].shape, 1) // block
    d = n // 2
    while d:
        keep = (lane & d) == 0
        out = list(rows)
        for a in range(n):
            if a & d:
                continue
            b = a + d
            out[a] = jnp.where(keep, rows[a], pltpu.roll(rows[b], d * block, 1))
            out[b] = jnp.where(keep, pltpu.roll(rows[a], width - d * block, 1), rows[b])
        rows = out
        d //= 2
    return rows


def kernel(dims, a_hbm, tm_hbm, l_hbm, h_hbm, out_ref,
           a_ref, a16_ref, tm_ref, l_ref, h_ref, am_ref, lg_ref, meta_ref, meta_smem,
           hsend, panel, psend, prep, ysend, yrecv, qsend, pfin,
           load_sem, meta_sem, h1_send, h1_recv, ring_send, ring_recv,
           p2_send, p2_recv, p3_send, p3_recv, p4_send, p4_recv):
    tiles, n_blk, share, width = dims
    half_tiles = tiles // 2
    p = lax.axis_index("pair")
    y = lax.axis_index("blk")
    x = lax.axis_index("rep")
    core = lax.rem(p, 2)
    zz = p // 2
    other_x = 1 - x
    sense = 1 - 2 * core
    up = lax.rem(y + sense + n_blk, n_blk)
    down = lax.rem(y - sense + n_blk, n_blk)

    loads = [
        pltpu.make_async_copy(tm_hbm, tm_ref, load_sem.at[0]),
        pltpu.make_async_copy(l_hbm, l_ref, load_sem.at[1]),
        pltpu.make_async_copy(h_hbm, h_ref, load_sem.at[2]),
        pltpu.make_async_copy(a_hbm, a_ref, load_sem.at[3]),
    ]
    loads[0].start()
    loads[3].start()
    loads[1].start()

    def plane(q):
        return jnp.where(lax.rem(q // 2 + zz, 2) == 0, x, other_x)

    barrier = pltpu.get_barrier_semaphore()

    @pl.loop(1, tiles)
    def _(j):
        q = lax.rem(p + j, tiles)
        pl.semaphore_signal(barrier, inc=1, device_id=(q, y, plane(q)), device_id_type=MESH)

    @pl.loop(1, n_blk)
    def _(j):
        pl.semaphore_signal(barrier, inc=1, device_id=(p, lax.rem(y + j, n_blk), x), device_id_type=MESH)

    pl.semaphore_signal(barrier, inc=1, device_id=(p, y, other_x), device_id_type=MESH)

    loads[0].wait()
    order_row, mask_row = tile_order_and_mask(tm_ref, p, tiles)
    meta_ref[0:1, 0:tiles] = order_row
    meta_ref[1:2, 0:tiles] = mask_row
    to_smem = pltpu.make_async_copy(meta_ref, meta_smem, meta_sem)
    to_smem.start()
    to_smem.wait()
    loads[3].wait()

    parity = lax.rem(core + x, 2)
    rows16 = pl.ds(pl.multiple_of(y * 16, 16), 16)
    for v in range(tiles):
        piece = a_ref[rows16, v * width:(v + 1) * width]
        a16_ref[v] = (piece.astype(F32) * meta_smem[1, v].astype(F32)).astype(BF16)
    for j in range(half_tiles):
        hsend[j] = a16_ref[meta_smem[0, 2 * j + lax.rem(parity + zz + j, 2)]]

    groups = 3
    per_group = tiles // groups
    step_cols = per_group * share

    def entry(n, pos):
        return 4 * groups * (pos // 4) + 4 * n + pos % 4

    def products():
        for j in range(half_tiles):
            kept = meta_smem[1, x * half_tiles + j].astype(F32)
            start = pl.multiple_of((x * half_tiles + j) * width, width)
            am_ref[:, j * width:(j + 1) * width] = (
                a_ref[:, pl.ds(start, width)].astype(F32) * kept).astype(BF16)
        loads[1].wait()
        lane = lax.broadcasted_iota(jnp.int32, (n_blk, 8, step_cols), 2) // (2 * share)
        for n in range(groups):
            for pos in range(per_group):
                lg_ref[n, pos * share:(pos + 1) * share, :] = l_ref[meta_smem[0, entry(n, pos)]]
            part = lax.dot_general(
                am_ref[...], lg_ref[n], (((1,), (1,)), ((), ())), preferred_element_type=F32)
            part = part.reshape(n_blk, 2, 8, step_cols)
            own = (lax.rem(lane, 2) == lax.rem(zz, 2)) == (x == 0)
            psend[n, 0] = jnp.where(own, part[:, 0], part[:, 1])
            psend[n, 1] = jnp.where(own, part[:, 1], part[:, 0])

    first_in = p < 2 * tiles // 3
    pl.when(first_in)(products)
    pl.semaphore_wait(barrier, tiles - 1 + n_blk - 1 + 1)

    group = half_tiles // 4

    @pl.when(x == 0)
    def _():
        pltpu.make_async_copy(hsend.at[zz], panel.at[x, y, 0], h1_recv.at[0]).start()

    @pl.when(x != 0)
    def _():
        pltpu.make_async_remote_copy(
            hsend.at[zz], panel.at[x, y, 0], h1_send, h1_recv.at[0],
            device_id=(2 * zz + parity, y, x), device_id_type=MESH).start()

    @pl.loop(1, half_tiles)
    def _(k):
        dest = lax.rem(zz + jnp.where(lax.rem(k, 2) == 1, (k + 1) // 2, half_tiles - k // 2), half_tiles)
        to_x = plane(2 * dest)
        pltpu.make_async_remote_copy(
            hsend.at[dest], panel.at[to_x, y, k], h1_send, h1_recv.at[k // group],
            device_id=(2 * dest + lax.rem(parity + zz + dest, 2), y, to_x), device_id_type=MESH).start()

    loads[2].start()

    pl.when(jnp.logical_not(first_in))(products)
    p2 = []
    for n in range(groups):
        p2.append(pltpu.make_async_remote_copy(
            psend.at[n, 1], prep.at[n], p2_send.at[n], p2_recv.at[n],
            device_id=(p, y, other_x), device_id_type=MESH))
        p2[n].start()

    copies = {}

    def slot(origin_x, origin_y, first, count):
        return panel.at[origin_x, lax.rem(origin_y + 2 * n_blk, n_blk), pl.ds(first, count)]

    def send(key, ref, to_y, to_x):
        which = len(copies)
        copies[key] = pltpu.make_async_remote_copy(
            ref, ref, ring_send.at[which], ring_recv.at[which],
            device_id=(p, to_y, to_x), device_id_type=MESH)
        copies[key].start()

    def spread(stream, step):
        over = stream < 3
        origin_x = other_x if stream == 4 else x
        last = stream % 2
        if step == 1:
            if stream == 4:
                copies[("swap",)].wait_recv()
            else:
                pieces_in(stream)
        if stream == 3 and step == 1:
            send(("swap",), slot(x, y, 3 * group, group), y, other_x)
        for d in range(2):
            if step == 5 and d != last:
                continue
            if step > 1:
                copies[(stream, step - 1, d)].wait_recv()
            origin = y - sense * (step - 1) if d == 0 else y + sense * (step - 1)
            ref = slot(origin_x, origin, min(stream, 3) * group, group)
            if step < 4 or (step == 4 and d == last):
                send((stream, step, d), ref, up if d == 0 else down, x)
            if over and (step > 1 or d == 0):
                send(("over", stream, step, d), ref, y, other_x)

    def particle_rows(n):
        p2[n].wait_recv()
        ysend[n] = psend[n, 0] + prep[n]

        @pl.loop(1, n_blk)
        def _(j):
            dest = lax.rem(y + sense * j + n_blk, n_blk)
            pltpu.make_async_remote_copy(
                ysend.at[n, dest], yrecv.at[n, y], p3_send.at[n], p3_recv.at[n],
                device_id=(p, dest, x), device_id_type=MESH).start()

        pltpu.make_async_copy(ysend.at[n, y], yrecv.at[n, y], p3_recv.at[n]).start()

    def particle_tiles(n):
        pltpu.make_async_copy(yrecv.at[n], yrecv.at[n], p3_recv.at[n]).wait()
        per = width // share
        for g in range(step_cols // width):
            rows = [yrecv[n, b, :, g * width:(g + 1) * width] for b in range(n_blk)]
            for k, row in enumerate(swap_lane_blocks(rows, share)):
                qsend[entry(n, g * per + k)] = row

        @pl.loop(0, per_group)
        def _(j):
            pos = lax.rem(j + p, per_group)
            q = 4 * groups * (pos // 4) + 4 * n + lax.rem(pos, 4)

            @pl.when(q != p)
            def _():
                pltpu.make_async_remote_copy(
                    qsend.at[q], pfin.at[p], p4_send, p4_recv,
                    device_id=(q, y, plane(q)), device_id_type=MESH).start()

            @pl.when(q == p)
            def _():
                pltpu.make_async_copy(qsend.at[q], pfin.at[p], p4_recv).start()

    def pieces_in(g):
        mine = panel.at[x, y, pl.ds(g * group, group)]
        pltpu.make_async_copy(mine, mine, h1_recv.at[g]).wait()

    spread(0, 1)
    spread(1, 1)
    particle_rows(0)
    spread(0, 2)
    spread(2, 1)
    particle_rows(1)
    spread(1, 2)
    particle_rows(2)
    spread(3, 1)
    spread(0, 3)
    spread(2, 2)
    particle_tiles(0)
    spread(1, 3)
    spread(4, 1)
    particle_tiles(1)
    spread(3, 2)
    spread(0, 4)
    spread(2, 3)
    particle_tiles(2)
    spread(1, 4)
    spread(4, 2)
    spread(3, 3)
    spread(0, 5)
    spread(2, 4)
    spread(1, 5)
    spread(4, 3)
    spread(3, 4)
    spread(2, 5)
    spread(4, 4)

    rows_out = out_ref.shape[0]

    def product(first, last, acc):
        for k in range(first, last):
            offset = (k + 1) // 2 if k % 2 else half_tiles - k // 2
            source = lax.rem(zz + 2 * half_tiles - offset, half_tiles)
            even = panel[core, :, k].reshape(width, width)
            odd = panel[1 - core, :, k].reshape(width, width)
            acc += jnp.dot(
                h_ref[:, pl.ds(pl.multiple_of(source * 2 * width, 2 * width), 2 * width)],
                jnp.concatenate([even, odd], axis=0), preferred_element_type=F32)
        return acc

    loads[2].wait()
    for key, copy in copies.items():
        if key[0] == "over":
            copy.wait_recv()
    acc = product(0, 3 * group, jnp.zeros((rows_out, width), F32))
    copies[(3, 4, 1)].wait_recv()
    copies[(4, 4, 0)].wait_recv()
    acc = product(3 * group, half_tiles, acc)
    pltpu.make_async_copy(pfin, pfin, p4_recv).wait()
    out_ref[...] = (acc + pfin[...].reshape(rows_out, width)).astype(BF16)

    @pl.when(x == 0)
    def _():
        sent = hsend.at[pl.ds(0, half_tiles - 1)]
        pltpu.make_async_copy(sent, sent, h1_send).wait()

    @pl.when(x != 0)
    def _():
        pltpu.make_async_copy(hsend, hsend, h1_send).wait()

    for copy in list(copies.values()) + p2:
        copy.wait_send()
    for n in range(groups):
        sent = ysend.at[n, pl.ds(0, n_blk - 1)]
        pltpu.make_async_copy(sent, sent, p3_send.at[n]).wait()
    sent = qsend.at[pl.ds(0, tiles - 1)]
    pltpu.make_async_copy(sent, sent, p4_send).wait()


def per_device(amplitudes, tile_map, ladder_ints, hole_ints):
    rows, total = amplitudes.shape
    tiles = tile_map.shape[0]
    width = total // tiles
    half_rows, _, share = ladder_ints.shape
    n_blk = width // share
    local_rows = hole_ints.shape[1]
    ladder = jnp.transpose(ladder_ints, (1, 2, 0))
    holes = hole_ints.reshape(tiles * local_rows, hole_ints.shape[2])
    dma = pltpu.SemaphoreType.DMA
    out = pl.pallas_call(
        functools.partial(kernel, (tiles, n_blk, share, width)),
        out_shape=jax.ShapeDtypeStruct((tiles * local_rows, width), BF16),
        in_specs=[pl.BlockSpec(memory_space=pl.ANY)] * 4,
        out_specs=pl.BlockSpec(memory_space=pltpu.VMEM),
        scratch_shapes=[
            pltpu.VMEM(amplitudes.shape, BF16),
            pltpu.VMEM((tiles, 16, width), BF16),
            pltpu.VMEM((tiles, tiles), jnp.int32),
            pltpu.VMEM(ladder.shape, BF16),
            pltpu.VMEM(holes.shape, BF16),
            pltpu.VMEM((rows, half_rows), BF16),
            pltpu.VMEM((3, tiles * share // 3, half_rows), BF16),
            pltpu.VMEM((8, 128), jnp.int32),
            pltpu.SMEM((8, 128), jnp.int32),
            pltpu.VMEM((tiles // 2, 16, width), BF16),
            pltpu.VMEM((2, n_blk, tiles // 2, 16, width), BF16),
            pltpu.VMEM((3, 2, n_blk, 8, tiles * share // 3), F32),
            pltpu.VMEM((3, n_blk, 8, tiles * share // 3), F32),
            pltpu.VMEM((3, n_blk, 8, tiles * share // 3), F32),
            pltpu.VMEM((3, n_blk, 8, tiles * share // 3), F32),
            pltpu.VMEM((tiles, 8, width), F32),
            pltpu.VMEM((tiles, 8, width), F32),
            dma((4,)), dma(()), dma(()), dma((4,)), dma((64,)), dma((64,)),
            dma((3,)), dma((3,)), dma((3,)), dma((3,)), dma(()), dma(()),
        ],
        compiler_params=pltpu.CompilerParams(
            collective_id=0, has_side_effects=True, vmem_limit_bytes=60 * 1024 * 1024),
        cost_estimate=pl.CostEstimate(flops=1_300_000_000, bytes_accessed=12_000_000, transcendentals=0),
    )(amplitudes, tile_map, ladder, holes)
    return out.reshape(1, tiles, local_rows, width)


def solution(mesh):
    placed = (P("pair", None), P(), P("rep", None, "blk"), P(None, ("blk", "rep"), None))
    return jax.shard_map(
        per_device,
        mesh=mesh,
        in_specs=placed,
        out_specs=P("pair", None, ("blk", "rep"), None),
        check_vma=False,
    )
```

```python
import functools

import jax
import jax.numpy as jnp
from jax import lax
from jax.experimental import pallas as pl
from jax.experimental.pallas import tpu as pltpu
from jax.sharding import PartitionSpec as P

MESH = pl.DeviceIdType.MESH
F32 = jnp.float32
BF16 = jnp.bfloat16


def tile_order_and_mask(tm_ref, pair_index, tiles):
    tm = tm_ref[...]
    lane = lax.broadcasted_iota(jnp.int32, (tiles, tiles), 1)
    sub = lax.broadcasted_iota(jnp.int32, (tiles, tiles), 0)
    score_row = jnp.sum(tm, axis=0, keepdims=True) * tiles + lane[:1]
    spread = jnp.broadcast_to(score_row, (tiles, tiles))
    score_col = jnp.sum(jnp.where(lane == sub, spread, 0), axis=1, keepdims=True)
    rank_col = jnp.sum((spread > score_col).astype(jnp.int32), axis=1, keepdims=True)
    order_row = jnp.sum(jnp.where(rank_col == lane, sub, 0), axis=0, keepdims=True)
    return order_row, tm_ref[pl.ds(pair_index, 1), :]


def swap_lane_blocks(rows, block):
    n = len(rows)
    width = n * block
    lane = lax.broadcasted_iota(jnp.int32, rows[0].shape, 1) // block
    d = n // 2
    while d:
        keep = (lane & d) == 0
        out = list(rows)
        for a in range(n):
            if a & d:
                continue
            b = a + d
            out[a] = jnp.where(keep, rows[a], pltpu.roll(rows[b], d * block, 1))
            out[b] = jnp.where(keep, pltpu.roll(rows[a], width - d * block, 1), rows[b])
        rows = out
        d //= 2
    return rows


def kernel(dims, a_hbm, tm_hbm, l_hbm, h_hbm, out_ref,
           a_ref, a16_ref, tm_ref, l_ref, h_ref, am_ref, lg_ref, meta_ref, meta_smem,
           hsend, panel, psend, prep, ysend, yrecv, qsend, pfin,
           load_sem, meta_sem, h1_send, h1_recv, ring_send, ring_recv,
           p2_send, p2_recv, p3_send, p3_recv, p4_send, p4_recv):
    tiles, n_blk, share, width = dims
    half_tiles = tiles // 2
    p = lax.axis_index("pair")
    y = lax.axis_index("blk")
    x = lax.axis_index("rep")
    core = lax.rem(p, 2)
    zz = p // 2
    other_x = 1 - x
    sense = 1 - 2 * core
    up = lax.rem(y + sense + n_blk, n_blk)
    down = lax.rem(y - sense + n_blk, n_blk)

    loads = [
        pltpu.make_async_copy(tm_hbm, tm_ref, load_sem.at[0]),
        pltpu.make_async_copy(l_hbm, l_ref, load_sem.at[1]),
        pltpu.make_async_copy(h_hbm, h_ref, load_sem.at[2]),
        pltpu.make_async_copy(a_hbm, a_ref, load_sem.at[3]),
    ]
    loads[0].start()
    loads[3].start()
    loads[1].start()

    def plane(q):
        return jnp.where(lax.rem(q // 2 + zz, 2) == 0, x, other_x)

    barrier = pltpu.get_barrier_semaphore()

    @pl.loop(1, tiles)
    def _(j):
        q = lax.rem(p + j, tiles)
        pl.semaphore_signal(barrier, inc=1, device_id=(q, y, plane(q)), device_id_type=MESH)

    @pl.loop(1, n_blk)
    def _(j):
        pl.semaphore_signal(barrier, inc=1, device_id=(p, lax.rem(y + j, n_blk), x), device_id_type=MESH)

    pl.semaphore_signal(barrier, inc=1, device_id=(p, y, other_x), device_id_type=MESH)

    loads[0].wait()
    order_row, mask_row = tile_order_and_mask(tm_ref, p, tiles)
    meta_ref[0:1, 0:tiles] = order_row
    meta_ref[1:2, 0:tiles] = mask_row
    to_smem = pltpu.make_async_copy(meta_ref, meta_smem, meta_sem)
    to_smem.start()
    to_smem.wait()
    loads[3].wait()

    parity = lax.rem(core + x, 2)
    rows16 = pl.ds(pl.multiple_of(y * 16, 16), 16)
    for v in range(tiles):
        piece = a_ref[rows16, v * width:(v + 1) * width]
        a16_ref[v] = (piece.astype(F32) * meta_smem[1, v].astype(F32)).astype(BF16)
    for j in range(half_tiles):
        hsend[j] = a16_ref[meta_smem[0, 2 * j + lax.rem(parity + zz + j, 2)]]

    groups = 3
    per_group = tiles // groups
    step_cols = per_group * share

    def entry(n, pos):
        return 4 * groups * (pos // 4) + 4 * n + pos % 4

    def products():
        for j in range(half_tiles):
            kept = meta_smem[1, x * half_tiles + j].astype(F32)
            start = pl.multiple_of((x * half_tiles + j) * width, width)
            am_ref[:, j * width:(j + 1) * width] = (
                a_ref[:, pl.ds(start, width)].astype(F32) * kept).astype(BF16)
        loads[1].wait()
        lane = lax.broadcasted_iota(jnp.int32, (n_blk, 8, step_cols), 2) // (2 * share)
        for n in range(groups):
            for pos in range(per_group):
                lg_ref[n, pos * share:(pos + 1) * share, :] = l_ref[meta_smem[0, entry(n, pos)]]
            part = lax.dot_general(
                am_ref[...], lg_ref[n], (((1,), (1,)), ((), ())), preferred_element_type=F32)
            part = part.reshape(n_blk, 2, 8, step_cols)
            own = (lax.rem(lane, 2) == lax.rem(zz, 2)) == (x == 0)
            psend[n, 0] = jnp.where(own, part[:, 0], part[:, 1])
            psend[n, 1] = jnp.where(own, part[:, 1], part[:, 0])

    first_in = p < 2 * tiles // 3
    pl.when(first_in)(products)
    pl.semaphore_wait(barrier, tiles - 1 + n_blk - 1 + 1)

    bounds = (0, 7, 14, 20, half_tiles)

    @pl.when(x == 0)
    def _():
        pltpu.make_async_copy(hsend.at[zz], panel.at[x, y, 0], h1_recv.at[0]).start()

    @pl.when(x != 0)
    def _():
        pltpu.make_async_remote_copy(
            hsend.at[zz], panel.at[x, y, 0], h1_send, h1_recv.at[0],
            device_id=(2 * zz + parity, y, x), device_id_type=MESH).start()

    @pl.loop(1, half_tiles)
    def _(k):
        dest = lax.rem(zz + jnp.where(lax.rem(k, 2) == 1, (k + 1) // 2, half_tiles - k // 2), half_tiles)
        to_x = plane(2 * dest)
        pltpu.make_async_remote_copy(
            hsend.at[dest], panel.at[to_x, y, k], h1_send, h1_recv.at[sum(jnp.where(k >= b, 1, 0) for b in bounds[1:4])],
            device_id=(2 * dest + lax.rem(parity + zz + dest, 2), y, to_x), device_id_type=MESH).start()

    loads[2].start()

    pl.when(jnp.logical_not(first_in))(products)
    p2 = []
    for n in range(groups):
        p2.append(pltpu.make_async_remote_copy(
            psend.at[n, 1], prep.at[n], p2_send.at[n], p2_recv.at[n],
            device_id=(p, y, other_x), device_id_type=MESH))
        p2[n].start()

    copies = {}

    def slot(origin_x, origin_y, first, count):
        return panel.at[origin_x, lax.rem(origin_y + 2 * n_blk, n_blk), pl.ds(first, count)]

    def send(key, ref, to_y, to_x):
        which = len(copies)
        copies[key] = pltpu.make_async_remote_copy(
            ref, ref, ring_send.at[which], ring_recv.at[which],
            device_id=(p, to_y, to_x), device_id_type=MESH)
        copies[key].start()

    def spread(stream, step):
        over = stream < 3
        origin_x = other_x if stream == 4 else x
        last = stream % 2
        if step == 1:
            if stream == 4:
                copies[("swap",)].wait_recv()
            else:
                pieces_in(stream)
        if stream == 3 and step == 1:
            send(("swap",), slot(x, y, bounds[3], bounds[4] - bounds[3]), y, other_x)
        for d in range(2):
            if step == 5 and d != last:
                continue
            if step > 1:
                copies[(stream, step - 1, d)].wait_recv()
            origin = y - sense * (step - 1) if d == 0 else y + sense * (step - 1)
            g = min(stream, 3)
            ref = slot(origin_x, origin, bounds[g], bounds[g + 1] - bounds[g])
            if step < 4 or (step == 4 and d == last):
                send((stream, step, d), ref, up if d == 0 else down, x)
            if over and (step > 1 or d == 0):
                send(("over", stream, step, d), ref, y, other_x)

    def particle_rows(n):
        p2[n].wait_recv()
        ysend[n] = psend[n, 0] + prep[n]

        @pl.loop(1, n_blk)
        def _(j):
            dest = lax.rem(y + sense * j + n_blk, n_blk)
            pltpu.make_async_remote_copy(
                ysend.at[n, dest], yrecv.at[n, y], p3_send.at[n], p3_recv.at[n],
                device_id=(p, dest, x), device_id_type=MESH).start()

        pltpu.make_async_copy(ysend.at[n, y], yrecv.at[n, y], p3_recv.at[n]).start()

    def particle_tiles(n):
        pltpu.make_async_copy(yrecv.at[n], yrecv.at[n], p3_recv.at[n]).wait()
        per = width // share
        for g in range(step_cols // width):
            rows = [yrecv[n, b, :, g * width:(g + 1) * width] for b in range(n_blk)]
            for k, row in enumerate(swap_lane_blocks(rows, share)):
                qsend[entry(n, g * per + k)] = row

        @pl.loop(0, per_group)
        def _(j):
            pos = lax.rem(j + p, per_group)
            q = 4 * groups * (pos // 4) + 4 * n + lax.rem(pos, 4)

            @pl.when(q != p)
            def _():
                pltpu.make_async_remote_copy(
                    qsend.at[q], pfin.at[p], p4_send, p4_recv,
                    device_id=(q, y, plane(q)), device_id_type=MESH).start()

            @pl.when(q == p)
            def _():
                pltpu.make_async_copy(qsend.at[q], pfin.at[p], p4_recv).start()

    def pieces_in(g):
        mine = panel.at[x, y, pl.ds(bounds[g], bounds[g + 1] - bounds[g])]
        pltpu.make_async_copy(mine, mine, h1_recv.at[g]).wait()

    spread(0, 1)
    spread(1, 1)
    particle_rows(0)
    spread(0, 2)
    spread(2, 1)
    particle_rows(1)
    spread(1, 2)
    particle_rows(2)
    spread(3, 1)
    spread(0, 3)
    spread(2, 2)
    particle_tiles(0)
    spread(1, 3)
    spread(4, 1)
    particle_tiles(1)
    spread(3, 2)
    spread(0, 4)
    spread(2, 3)
    particle_tiles(2)
    spread(1, 4)
    spread(4, 2)
    spread(3, 3)
    spread(0, 5)
    spread(2, 4)
    spread(1, 5)
    spread(4, 3)
    spread(3, 4)
    spread(2, 5)
    spread(4, 4)

    rows_out = out_ref.shape[0]

    def product(first, last, acc):
        for k in range(first, last):
            offset = (k + 1) // 2 if k % 2 else half_tiles - k // 2
            source = lax.rem(zz + 2 * half_tiles - offset, half_tiles)
            even = panel[core, :, k].reshape(width, width)
            odd = panel[1 - core, :, k].reshape(width, width)
            acc += jnp.dot(
                h_ref[:, pl.ds(pl.multiple_of(source * 2 * width, 2 * width), 2 * width)],
                jnp.concatenate([even, odd], axis=0), preferred_element_type=F32)
        return acc

    loads[2].wait()
    for key, copy in copies.items():
        if key[0] == "over":
            copy.wait_recv()
    acc = product(0, bounds[3], jnp.zeros((rows_out, width), F32))
    copies[(3, 4, 1)].wait_recv()
    copies[(4, 4, 0)].wait_recv()
    acc = product(bounds[3], half_tiles, acc)
    pltpu.make_async_copy(pfin, pfin, p4_recv).wait()
    out_ref[...] = (acc + pfin[...].reshape(rows_out, width)).astype(BF16)

    @pl.when(x == 0)
    def _():
        sent = hsend.at[pl.ds(0, half_tiles - 1)]
        pltpu.make_async_copy(sent, sent, h1_send).wait()

    @pl.when(x != 0)
    def _():
        pltpu.make_async_copy(hsend, hsend, h1_send).wait()

    for copy in list(copies.values()) + p2:
        copy.wait_send()
    for n in range(groups):
        sent = ysend.at[n, pl.ds(0, n_blk - 1)]
        pltpu.make_async_copy(sent, sent, p3_send.at[n]).wait()
    sent = qsend.at[pl.ds(0, tiles - 1)]
    pltpu.make_async_copy(sent, sent, p4_send).wait()


def per_device(amplitudes, tile_map, ladder_ints, hole_ints):
    rows, total = amplitudes.shape
    tiles = tile_map.shape[0]
    width = total // tiles
    half_rows, _, share = ladder_ints.shape
    n_blk = width // share
    local_rows = hole_ints.shape[1]
    ladder = jnp.transpose(ladder_ints, (1, 2, 0))
    holes = hole_ints.reshape(tiles * local_rows, hole_ints.shape[2])
    dma = pltpu.SemaphoreType.DMA
    out = pl.pallas_call(
        functools.partial(kernel, (tiles, n_blk, share, width)),
        out_shape=jax.ShapeDtypeStruct((tiles * local_rows, width), BF16),
        in_specs=[pl.BlockSpec(memory_space=pl.ANY)] * 4,
        out_specs=pl.BlockSpec(memory_space=pltpu.VMEM),
        scratch_shapes=[
            pltpu.VMEM(amplitudes.shape, BF16),
            pltpu.VMEM((tiles, 16, width), BF16),
            pltpu.VMEM((tiles, tiles), jnp.int32),
            pltpu.VMEM(ladder.shape, BF16),
            pltpu.VMEM(holes.shape, BF16),
            pltpu.VMEM((rows, half_rows), BF16),
            pltpu.VMEM((3, tiles * share // 3, half_rows), BF16),
            pltpu.VMEM((8, 128), jnp.int32),
            pltpu.SMEM((8, 128), jnp.int32),
            pltpu.VMEM((tiles // 2, 16, width), BF16),
            pltpu.VMEM((2, n_blk, tiles // 2, 16, width), BF16),
            pltpu.VMEM((3, 2, n_blk, 8, tiles * share // 3), F32),
            pltpu.VMEM((3, n_blk, 8, tiles * share // 3), F32),
            pltpu.VMEM((3, n_blk, 8, tiles * share // 3), F32),
            pltpu.VMEM((3, n_blk, 8, tiles * share // 3), F32),
            pltpu.VMEM((tiles, 8, width), F32),
            pltpu.VMEM((tiles, 8, width), F32),
            dma((4,)), dma(()), dma(()), dma((4,)), dma((64,)), dma((64,)),
            dma((3,)), dma((3,)), dma((3,)), dma((3,)), dma(()), dma(()),
        ],
        compiler_params=pltpu.CompilerParams(
            collective_id=0, has_side_effects=True, vmem_limit_bytes=60 * 1024 * 1024),
        cost_estimate=pl.CostEstimate(flops=1_300_000_000, bytes_accessed=12_000_000, transcendentals=0),
    )(amplitudes, tile_map, ladder, holes)
    return out.reshape(1, tiles, local_rows, width)


def solution(mesh):
    placed = (P("pair", None), P(), P("rep", None, "blk"), P(None, ("blk", "rep"), None))
    return jax.shard_map(
        per_device,
        mesh=mesh,
        in_specs=placed,
        out_specs=P("pair", None, ("blk", "rep"), None),
        check_vma=False,
    )
```
